32 devices in a mesh: dp: 4 (over z), seq: 8 (over y, x, core).
Axes of the slice: x: 2, y: 2, z: 4, core: 2. Of those that a mesh axis runs over, the one named last changes fastest.
Arguments:
- tokens: bfloat16 [8192, 2048], P(('dp', 'seq')), may hold values from -6 to 6
- weights: bfloat16 [2048, 24576], P('dp'), may hold values from -1 to 1
- ln_gain: float32 [2, 2048], replicated, may hold values from 0.5 to 1.5
- ln_bias: float32 [2, 2048], replicated, may hold values from -1 to 1
- doc_starts: int32 [4, 4], P('dp'), may hold values from 0 to 2047, as said below
- cotangent: bfloat16 [8192, 2048], P(('dp', 'seq')), may hold values from -6 to 6
Outputs:
- output: bfloat16 [8192, 2048], P(('dp', 'seq'))
- grad_tokens: float32 [8192, 2048], P(('dp', 'seq'))
- grad_weights: float32 [2048, 24576], P(('dp', 'seq'))
- grad_gain: float32 [2, 2048], replicated
- grad_bias: float32 [2, 2048], replicated
The draws below stay inside these ranges and needn't reach their ends.
Inputs may be any that keep to these rules, and one draw needn't show every extreme that they name: `doc_starts`: the first entry of each row is 0; entries do not fall along a row and may repeat.
All inputs are finite; a program needn't handle non-finite values.
Results may differ from the reference program's by a relative error of at most 0.014.
The reference program's roundings to bfloat16 on the way count: a program that leaves them out, or rounds other values in their place, can miss the bound.
Values may be sent and summed in bfloat16 or wider, within the bound.
A program may use at most 832 MiB of HBM per device.

```python
import jax
import jax.numpy as jnp
from jax import lax

D = 2048
HEADS = 8
QK = 256
VD = 512
FF = 4096
TOK_DEV = 256
DOCS = 4
LENGTH = 2048
ROWS = 4
TOKENS = 8192
COLS = 24576
N_SEQ = 8


def draw_doc_starts(key, part):
    later_starts = jax.random.randint(key, (ROWS, DOCS - 1), 1, LENGTH)
    later_starts = jnp.sort(later_starts, axis=1).astype(jnp.int32)
    later_starts = later_starts.at[0, DOCS - 2].set(LENGTH - 1)
    return jnp.concatenate([jnp.zeros((ROWS, 1), jnp.int32), later_starts], axis=1)


def draw_weights(key, part):
    scale = 1.0 / D ** 0.5
    values = jnp.clip(jax.random.normal(key, (D, COLS), jnp.float32), -6.0, 6.0)
    return (values * scale).astype(jnp.bfloat16)


def shard_levels(own_key, dims, pieces, least, largest):
    factor_of, own = 1.0, jax.random.fold_in(own_key, 6)
    for dim, parts in pieces:
        heights = jnp.exp(jax.random.uniform(jax.random.fold_in(own, dim), (parts,), jnp.float32, least / len(pieces), largest / len(pieces)))
        factor_of = factor_of * jnp.repeat(heights, dims[dim] // parts).reshape([-1 if axis == dim else 1 for axis in range(len(dims))])
    return factor_of


def gaussian(key, extent, scale, most, split=(), kind=jnp.bfloat16):
    array = jax.random.normal(key, extent, jnp.float32) * scale
    if len(split) > 0:
        array = shard_levels(key, extent, split, -0.22, 0.18) * array
    return jnp.clip(array, min=-most, max=most).astype(kind)


def setup_inputs(seed: int = 0) -> dict:
    key_list = jax.random.split(jax.random.key(seed), 7)
    return {
        "tokens": gaussian(key_list[0], (TOKENS, D), 1.0, 6.0, ((0, 32),)),
        "weights": draw_weights(jax.random.fold_in(key_list[6], 71), 0),
        "ln_gain": jnp.clip(1.0 + 0.1 * jax.random.normal(key_list[2], (2, D), jnp.float32), 0.5, 1.5),
        "ln_bias": gaussian(key_list[3], (2, D), 0.2, 1.0, (), jnp.float32),
        "doc_starts": draw_doc_starts(jax.random.fold_in(key_list[6], 71), 0),
        "cotangent": gaussian(key_list[5], (TOKENS, D), 1.0, 6.0, ((0, 32),)),
    }


@jax.custom_vjp
def low(v):
    return lax.optimization_barrier(v.astype(jnp.bfloat16)).astype(jnp.float32)

@jax.custom_vjp
def low_back(v):
    return v

def low_keep(v):
    return (low(v), None)

def low_pass(kept, grad):
    return (grad,)

def back_keep(v):
    return (v, None)

def back_low(kept, grad):
    return (low(grad),)
low.defvjp(low_keep, low_pass)
low_back.defvjp(back_keep, back_low)
norm_eps = 1e-05
highest = lax.Precision.HIGHEST

def matmul(left, right):
    return jnp.dot(left, right, precision=highest, preferred_element_type=jnp.float32)

def matmul_trans(left, right):
    return lax.dot_general(left, right, (((1,), (1,)), ((), ())), precision=highest, preferred_element_type=jnp.float32)

def layer_norm(values, gain, shift):
    centre = lax.optimization_barrier(jnp.mean(values, axis=-1, keepdims=True))
    centred = values - centre
    spread = lax.optimization_barrier(jnp.mean(centred * centred, axis=-1, keepdims=True))
    return centred * lax.rsqrt(spread + norm_eps) * gain + shift

def group_norm(values):
    centre = lax.optimization_barrier(jnp.mean(values, axis=-1, keepdims=True))
    centred = values - centre
    spread = lax.optimization_barrier(jnp.mean(centred * centred, axis=-1, keepdims=True))
    return centred * lax.rsqrt(spread + norm_eps)

def gelu_tanh(values):
    return jax.nn.gelu(values, approximate=True)

def rotate(values, positions, heads_count):
    length = values.shape[0]
    shaped = values.reshape(length, heads_count, -1)
    half_size = shaped.shape[-1] // 2
    inverse = 10000.0 ** (-(jnp.arange(half_size, dtype=jnp.float32) / half_size))
    angles = positions.astype(jnp.float32)[:, None] * inverse[None, :]
    cosine = jnp.cos(angles)[:, None, :]
    sine = jnp.sin(angles)[:, None, :]
    front = shaped[..., :half_size]
    back_half = shaped[..., half_size:]
    turned = jnp.concatenate([front * cosine - back_half * sine, back_half * cosine + front * sine], axis=-1)
    return turned.reshape(length, -1)

def decay_tables(segs, seg_prev, heads_count):
    length = segs.shape[0]
    logs = jnp.log1p(-2.0 ** (-5.0 - jnp.arange(heads_count, dtype=jnp.float32)))
    local = jnp.arange(length, dtype=jnp.int32)
    gap = (local[:, None] - local[None, :]).astype(jnp.float32)
    same = (segs[:, None] == segs[None, :]) & (local[:, None] >= local[None, :])
    within = jnp.where(same[None], jnp.exp(jnp.where(same[None], gap[None] * logs[:, None, None], 0.0)), 0.0)
    reach = jnp.where((segs == seg_prev)[None, :], jnp.exp((local + 1).astype(jnp.float32)[None, :] * logs[:, None]), 0.0)
    ending = jnp.where((segs == segs[-1])[None, :], jnp.exp((length - 1 - local).astype(jnp.float32)[None, :] * logs[:, None]), 0.0)
    carry = jnp.where(segs[-1] == seg_prev, jnp.exp(length * logs), 0.0)
    return (within, reach.T, ending.T, carry)

def layer_row(row_tokens, weights, ln_gain, ln_bias, starts):
    length = row_tokens.shape[0]
    query_width = HEADS * QK
    value_width = HEADS * VD
    mixer_cols = 2 * query_width + 2 * value_width
    ffn_end = mixer_cols + FF
    out_end = ffn_end + value_width
    positions = jnp.arange(length, dtype=jnp.int32)
    segs = lax.optimization_barrier(jnp.sum((starts[None, :] <= positions[:, None]).astype(jnp.int32), axis=1)).astype(jnp.int32)
    first = low(layer_norm(row_tokens, ln_gain[0], ln_bias[0]))
    project = matmul(first, weights[:, :mixer_cols])
    query = low(rotate(low_back(project[:, :query_width]), positions, HEADS))
    keys = low(rotate(low_back(project[:, query_width:2 * query_width]), positions, HEADS))
    values = low(low_back(project[:, 2 * query_width:2 * query_width + value_width]))
    gate = low_back(project[:, 2 * query_width + value_width:mixer_cols])
    seg_blocks = segs.reshape(N_SEQ, TOK_DEV)
    seg_before = jnp.concatenate([jnp.zeros((1,), jnp.int32), seg_blocks[:-1, -1].astype(jnp.int32)])

    def retain(state, items):
        query_block, key_block, value_block, seg_block, seg_prev = items
        within, reach, ending, carry = decay_tables(seg_block, seg_prev, HEADS)
        scores = low_back(jnp.einsum('thd,shd->hts', query_block, key_block, precision=highest))
        attn_weights = low(scores * within)
        intra = jnp.einsum('hts,shv->thv', attn_weights, value_block, precision=highest)
        across = jnp.einsum('thd,hdv->thv', query_block, low(state), precision=highest) * reach[:, :, None]
        own_state = jnp.einsum('thd,thv->hdv', key_block * ending[:, :, None], value_block, precision=highest)
        return (own_state + carry[:, None, None] * state, intra + across)
    state_zero = jnp.zeros((HEADS, QK, VD), jnp.float32)
    blocks = (query.reshape(N_SEQ, TOK_DEV, HEADS, QK), keys.reshape(N_SEQ, TOK_DEV, HEADS, QK), values.reshape(N_SEQ, TOK_DEV, HEADS, VD), seg_blocks, seg_before)
    mixed = lax.scan(jax.checkpoint(retain), state_zero, blocks)[1]
    mixed = low_back(mixed.reshape(length, HEADS, VD))
    grouped = group_norm(mixed).reshape(length, value_width)
    gated = low(jax.nn.silu(gate) * grouped)
    hidden = row_tokens + low_back(matmul_trans(gated, weights[:, ffn_end:out_end]))
    second = low(layer_norm(hidden, ln_gain[1], ln_bias[1]))
    inner = low_back(matmul(second, weights[:, mixer_cols:ffn_end]))
    active = low(gelu_tanh(inner))
    return hidden + low_back(matmul_trans(active, weights[:, out_end:]))

def reference(tokens, weights, ln_gain, ln_bias, doc_starts, cotangent):
    weights_wide = weights.astype(jnp.float32)
    row_inputs = tokens.astype(jnp.float32).reshape(ROWS, LENGTH, D)
    row_cots = cotangent.astype(jnp.float32).reshape(ROWS, LENGTH, D)

    def one_row(totals, items):
        row_tokens, row_cot, starts = items

        def forward(inputs, matrix, gains, shifts):
            return layer_row(inputs, matrix, gains, shifts, starts)
        outputs, pullback = jax.vjp(forward, row_tokens, weights_wide, ln_gain, ln_bias)
        grad_row, grad_matrix, grad_gains, grad_shifts = pullback(row_cot)
        totals = (totals[0] + grad_matrix, totals[1] + grad_gains, totals[2] + grad_shifts)
        return (totals, (outputs, grad_row))
    start_totals = (jnp.zeros_like(weights_wide), jnp.zeros_like(ln_gain), jnp.zeros_like(ln_bias))
    totals, produced = lax.scan(one_row, start_totals, (row_inputs, row_cots, doc_starts))
    outputs, grad_rows = produced
    return (outputs.reshape(TOKENS, D).astype(jnp.bfloat16), grad_rows.reshape(TOKENS, D), totals[0], totals[1], totals[2])
```

```python
import jax
import jax.numpy as jnp
from jax import lax
from jax.sharding import PartitionSpec as P

HEADS = 8
QK = 256
VD = 512
FF = 4096


norm_eps = 1e-05
highest = lax.Precision.HIGHEST
f32 = jnp.float32
bf16 = jnp.bfloat16


def prefix(x, axis, combine, identity, reverse):
    devices, place = (lax.axis_size(axis), lax.axis_index(axis))
    everything = jax.tree.map(lambda part: lax.all_gather(part, axis), x)
    start = jax.tree.map(
        lambda part, zero: jnp.broadcast_to(jnp.asarray(zero, part.dtype), part.shape), x, identity
    )

    def step(k, before):
        at = devices - 1 - k if reverse else k
        reached = at > place if reverse else at < place
        new = combine(before, jax.tree.map(lambda part: part[at], everything))
        return jax.tree.map(lambda a, b: jnp.where(reached, a, b), new, before)

    return lax.fori_loop(0, devices, step, start)


def layer_norm(values, gain, shift):
    centre = jnp.mean(values, axis=-1, keepdims=True)
    centred = values - centre
    spread = jnp.mean(centred * centred, axis=-1, keepdims=True)
    return centred * lax.rsqrt(spread + norm_eps) * gain + shift


def group_norm(values):
    centre = jnp.mean(values, axis=-1, keepdims=True)
    centred = values - centre
    spread = jnp.mean(centred * centred, axis=-1, keepdims=True)
    return centred * lax.rsqrt(spread + norm_eps)


def gelu_tanh(values):
    return jax.nn.gelu(values, approximate=True)


def gating(gate_values, normed):
    return jax.nn.silu(gate_values) * normed


def rotate(values, positions, heads_count):
    length = values.shape[0]
    shaped = values.reshape(length, heads_count, -1)
    half_size = shaped.shape[-1] // 2
    inverse = 10000.0 ** (-(jnp.arange(half_size, dtype=jnp.float32) / half_size))
    angles = positions.astype(jnp.float32)[:, None] * inverse[None, :]
    cosine = jnp.cos(angles)[:, None, :]
    sine = jnp.sin(angles)[:, None, :]
    front = shaped[..., :half_size]
    back_half = shaped[..., half_size:]
    turned = jnp.concatenate(
        [front * cosine - back_half * sine, back_half * cosine + front * sine], axis=-1
    )
    return turned.reshape(length, -1)


def head_logs():
    return jnp.log1p(-(2.0 ** (-5.0 - jnp.arange(HEADS, dtype=jnp.float32))))


def decay_tables(segs, seg_prev, logs):
    length = segs.shape[0]
    local = jnp.arange(length, dtype=jnp.int32)
    gap = (local[:, None] - local[None, :]).astype(jnp.float32)
    same = (segs[:, None] == segs[None, :]) & (local[:, None] >= local[None, :])
    within = jnp.where(
        same[None], jnp.exp(jnp.where(same[None], gap[None] * logs[:, None, None], 0.0)), 0.0
    )
    reach = jnp.where(
        (segs == seg_prev)[None, :],
        jnp.exp((local + 1).astype(jnp.float32)[None, :] * logs[:, None]),
        0.0,
    )
    ending = jnp.where(
        (segs == segs[-1])[None, :],
        jnp.exp((length - 1 - local).astype(jnp.float32)[None, :] * logs[:, None]),
        0.0,
    )
    carry = jnp.where(segs[-1] == seg_prev, jnp.exp(length * logs), 0.0)
    return (within, reach.T, ending.T, carry)


def combine_states(earlier, later):
    return (later[0] + later[1][:, None, None] * earlier[0], earlier[1] * later[1])


def contract_last(left, right):
    return lax.dot_general(
        left, right, (((1,), (1,)), ((), ())), preferred_element_type=jnp.float32
    )


def per_device_spread(tokens, weights, ln_gain, ln_bias, doc_starts, cotangent):
    full = lax.all_gather(weights, "dp", axis=0, tiled=True)
    query_width = HEADS * QK
    value_width = HEADS * VD
    mixer_cols = 2 * query_width + 2 * value_width
    ffn_end = mixer_cols + FF
    out_end = ffn_end + value_width
    block = tokens.shape[0]
    offset = lax.axis_index("seq") * block
    positions = offset + jnp.arange(block, dtype=jnp.int32)
    starts = doc_starts[0]
    segs = jnp.sum((starts[None, :] <= positions[:, None]).astype(jnp.int32), axis=1)
    seg_prev = jnp.sum((starts <= offset - 1).astype(jnp.int32))
    within, reach, ending, carry = decay_tables(segs, seg_prev, head_logs())
    inputs = tokens.astype(jnp.float32)
    first, first_pull = jax.vjp(layer_norm, inputs, ln_gain[0], ln_bias[0])
    first_low = first.astype(jnp.bfloat16)
    project = jnp.dot(first_low, full[:, :mixer_cols], preferred_element_type=jnp.float32)

    def rotate_here(values):
        return rotate(values, positions, HEADS)

    query_rot, rotate_pull = jax.vjp(rotate_here, project[:, :query_width])
    query_low = query_rot.astype(jnp.bfloat16).reshape(block, HEADS, QK)
    key_low = (
        rotate_here(project[:, query_width : 2 * query_width])
        .astype(jnp.bfloat16)
        .reshape(block, HEADS, QK)
    )
    value_low = (
        project[:, 2 * query_width : 2 * query_width + value_width]
        .astype(jnp.bfloat16)
        .reshape(block, HEADS, VD)
    )
    gate_raw = project[:, 2 * query_width + value_width : mixer_cols]
    scores = jnp.einsum("thd,shd->hts", query_low, key_low, preferred_element_type=jnp.float32)
    attn_low = (scores * within).astype(jnp.bfloat16)
    intra = jnp.einsum("hts,shv->thv", attn_low, value_low, preferred_element_type=jnp.float32)
    key_scaled = key_low.astype(jnp.float32) * ending[:, :, None]
    value_wide = value_low.astype(jnp.float32)
    own_state = jnp.einsum("thd,thv->hdv", key_scaled, value_wide, precision=highest)
    incoming = prefix(
        (own_state, carry),
        "seq",
        combine_states,
        (jnp.zeros_like(own_state), jnp.ones_like(carry)),
        False,
    )[0]
    state_low = incoming.astype(jnp.bfloat16)
    across = (
        jnp.einsum("thd,hdv->thv", query_low, state_low, preferred_element_type=jnp.float32)
        * reach[:, :, None]
    )
    mixed = intra + across
    grouped, group_pull = jax.vjp(group_norm, mixed)
    gated, gating_pull = jax.vjp(gating, gate_raw, grouped.reshape(block, value_width))
    gated_low = gated.astype(jnp.bfloat16)
    hidden = inputs + contract_last(gated_low, full[:, ffn_end:out_end])
    second, second_pull = jax.vjp(layer_norm, hidden, ln_gain[1], ln_bias[1])
    second_low = second.astype(jnp.bfloat16)
    inner = jnp.dot(second_low, full[:, mixer_cols:ffn_end], preferred_element_type=jnp.float32)
    active, active_pull = jax.vjp(gelu_tanh, inner)
    active_low = active.astype(jnp.bfloat16)
    result = (hidden + contract_last(active_low, full[:, out_end:])).astype(jnp.bfloat16)
    grad_active = jnp.dot(cotangent, full[:, out_end:], preferred_element_type=jnp.float32)
    grad_inner_low = active_pull(grad_active)[0].astype(jnp.bfloat16)
    grad_second = contract_last(grad_inner_low, full[:, mixer_cols:ffn_end])
    grad_hidden_ln, gain_two, bias_two = second_pull(grad_second)
    grad_hidden = cotangent.astype(jnp.float32) + grad_hidden_ln
    grad_branch_low = grad_hidden.astype(jnp.bfloat16)
    grad_gated = jnp.dot(
        grad_branch_low, full[:, ffn_end:out_end], preferred_element_type=jnp.float32
    )
    grad_gate, grad_grouped = gating_pull(grad_gated)
    grad_mixed_low = group_pull(grad_grouped.reshape(block, HEADS, VD))[0].astype(jnp.bfloat16)
    grad_attn = jnp.einsum(
        "thv,shv->hts", grad_mixed_low, value_low, preferred_element_type=jnp.float32
    )
    grad_scores_low = (grad_attn * within).astype(jnp.bfloat16)
    grad_query = jnp.einsum(
        "hts,shd->thd", grad_scores_low, key_low, preferred_element_type=jnp.float32
    )
    grad_query = (
        grad_query
        + jnp.einsum("thv,hdv->thd", grad_mixed_low, state_low, preferred_element_type=jnp.float32)
        * reach[:, :, None]
    )
    grad_key = jnp.einsum(
        "hts,thd->shd", grad_scores_low, query_low, preferred_element_type=jnp.float32
    )
    grad_value = jnp.einsum(
        "hts,thv->shv", attn_low, grad_mixed_low, preferred_element_type=jnp.float32
    )
    grad_state = jnp.einsum(
        "thd,thv->hdv",
        query_low.astype(jnp.float32) * reach[:, :, None],
        grad_mixed_low.astype(jnp.float32),
        precision=highest,
    )
    grad_own = prefix(
        (grad_state, carry),
        "seq",
        combine_states,
        (jnp.zeros_like(grad_state), jnp.ones_like(carry)),
        True,
    )[0]
    grad_key = (
        grad_key
        + jnp.einsum("thv,hdv->thd", value_wide, grad_own, precision=highest) * ending[:, :, None]
    )
    grad_value = grad_value + jnp.einsum("thd,hdv->thv", key_scaled, grad_own, precision=highest)
    grad_query_raw = rotate_pull(grad_query.reshape(block, query_width))[0]
    grad_key_raw = rotate_pull(grad_key.reshape(block, query_width))[0]
    grad_project_low = jnp.concatenate(
        [
            grad_query_raw.astype(jnp.bfloat16),
            grad_key_raw.astype(jnp.bfloat16),
            grad_value.reshape(block, value_width).astype(jnp.bfloat16),
            grad_gate.astype(jnp.bfloat16),
        ],
        axis=1,
    )
    grad_first = contract_last(grad_project_low, full[:, :mixer_cols])
    grad_input_ln, gain_one, bias_one = first_pull(grad_first)
    grad_tokens = grad_hidden + grad_input_ln
    contract = (((0,), (0,)), ((), ()))
    pieces = [
        lax.dot_general(first_low, grad_project_low, contract, preferred_element_type=jnp.float32),
        lax.dot_general(second_low, grad_inner_low, contract, preferred_element_type=jnp.float32),
        lax.dot_general(grad_branch_low, gated_low, contract, preferred_element_type=jnp.float32),
        lax.dot_general(cotangent, active_low, contract, preferred_element_type=jnp.float32),
    ]
    grad_weights = lax.psum_scatter(
        jnp.concatenate(pieces, axis=1), ("dp", "seq"), scatter_dimension=0, tiled=True
    )
    grad_gain, grad_bias = lax.psum(
        (jnp.stack([gain_one, gain_two]), jnp.stack([bias_one, bias_two])), ("dp", "seq")
    )
    return (result, grad_tokens, grad_weights, grad_gain, grad_bias)


def sections(n_seq):
    widths = (HEADS * QK, HEADS * QK, HEADS * VD, HEADS * VD, FF, HEADS * VD, FF)
    start, out = 0, []
    for width in widths:
        out.append((start, width // n_seq))
        start += width
    return out


def per_device_heads(tokens, weights, ln_gain, ln_bias, doc_starts, cotangent):
    n_seq, place = lax.axis_size("seq"), lax.axis_index("seq")
    heads = HEADS // n_seq
    block = tokens.shape[0]
    length = block * n_seq
    secs = sections(n_seq)

    def gather_weights(which):
        part = jnp.concatenate(
            [
                lax.dynamic_slice_in_dim(weights, start + place * width, width, axis=1)
                for start, width in (secs[i] for i in which)
            ],
            axis=1,
        )
        return lax.all_gather(part, "dp", axis=0, tiled=True)

    w_qk = gather_weights((0, 1))
    w_v = gather_weights((2,))
    w_g = gather_weights((3,))
    w_out = gather_weights((5,))
    w_in = gather_weights((4,))
    w_down = gather_weights((6,))

    def row_gather(part):
        return lax.all_gather(part, "seq", axis=0, tiled=True)

    def row_scatter(full):
        return lax.psum_scatter(
            full.astype(bf16), "seq", scatter_dimension=0, tiled=True
        ).astype(f32)

    positions = jnp.arange(length, dtype=jnp.int32)
    starts = doc_starts[0]
    segs = jnp.sum((starts[None, :] <= positions[:, None]).astype(jnp.int32), axis=1)
    seg_blocks = segs.reshape(n_seq, block)
    seg_before = jnp.concatenate([jnp.zeros((1,), jnp.int32), seg_blocks[:-1, -1]])
    inputs = tokens.astype(f32)
    first, first_pull = jax.vjp(layer_norm, inputs, ln_gain[0], ln_bias[0])
    first_low = row_gather(first.astype(bf16))
    cot_low = row_gather(cotangent)
    qk_raw = jnp.dot(first_low, w_qk, preferred_element_type=f32)

    def rotate_here(values):
        return rotate(values, positions, heads)

    query_rot, rotate_pull = jax.vjp(rotate_here, qk_raw[:, : heads * QK])

    def blocked(values):
        return values.reshape(n_seq, block, heads, -1)

    query_low = blocked(query_rot.astype(bf16))
    key_low = blocked(rotate_here(qk_raw[:, heads * QK :]).astype(bf16))
    value_low = blocked(jnp.dot(first_low, w_v, preferred_element_type=f32).astype(bf16))
    gate_raw = jnp.dot(first_low, w_g, preferred_element_type=f32)
    logs = lax.dynamic_slice_in_dim(head_logs(), place * heads, heads)
    within, reach, ending, carry = jax.vmap(decay_tables, (0, 0, None))(
        seg_blocks, seg_before, logs
    )
    scores = jnp.einsum("bthd,bshd->bhts", query_low, key_low, preferred_element_type=f32)
    attn_low = (scores * within).astype(bf16)
    intra = jnp.einsum("bhts,bshv->bthv", attn_low, value_low, preferred_element_type=f32)
    key_scaled = key_low.astype(f32) * ending[..., None]
    value_wide = value_low.astype(f32)
    own_state = jnp.einsum("bthd,bthv->bhdv", key_scaled, value_wide, precision=highest)
    state = jnp.zeros_like(own_state[0])
    states = []
    for b in range(n_seq):
        states.append(state.astype(bf16))
        state = own_state[b] + carry[b][:, None, None] * state
    state_low = jnp.stack(states)
    across = (
        jnp.einsum("bthd,bhdv->bthv", query_low, state_low, preferred_element_type=f32)
        * reach[..., None]
    )
    mixed = (intra + across).reshape(length, heads, VD)
    grouped, group_pull = jax.vjp(group_norm, mixed)
    gated, gating_pull = jax.vjp(gating, gate_raw, grouped.reshape(length, heads * VD))
    gated_low = gated.astype(bf16)
    hidden = inputs + row_scatter(contract_last(gated_low, w_out))
    second, second_pull = jax.vjp(layer_norm, hidden, ln_gain[1], ln_bias[1])
    second_low = row_gather(second.astype(bf16))
    inner = jnp.dot(second_low, w_in, preferred_element_type=f32)
    active, active_pull = jax.vjp(gelu_tanh, inner)
    active_low = active.astype(bf16)
    result = (hidden + row_scatter(contract_last(active_low, w_down))).astype(bf16)
    contract = (((0,), (0,)), ((), ()))

    def weight_grad(left, right):
        return lax.psum_scatter(
            lax.dot_general(left, right, contract, preferred_element_type=f32).astype(bf16),
            "dp",
            scatter_dimension=0,
            tiled=True,
        )

    def spread(grad):
        return lax.all_to_all(grad, "seq", 0, 1, tiled=True).astype(f32)

    g_down = weight_grad(cot_low, active_low)
    grad_active = jnp.dot(cot_low, w_down, preferred_element_type=f32)
    grad_inner_low = active_pull(grad_active)[0].astype(bf16)
    grad_second = row_scatter(contract_last(grad_inner_low, w_in))
    g_in = weight_grad(second_low, grad_inner_low)
    grad_hidden_ln, gain_two, bias_two = second_pull(grad_second)
    grad_hidden = cotangent.astype(f32) + grad_hidden_ln
    grad_branch_low = row_gather(grad_hidden.astype(bf16))
    g_out = weight_grad(grad_branch_low, gated_low)
    grad_gated = jnp.dot(grad_branch_low, w_out, preferred_element_type=f32)
    grad_gate, grad_grouped = gating_pull(grad_gated)
    grad_gate_low = grad_gate.astype(bf16)
    g_g = weight_grad(first_low, grad_gate_low)
    grad_mixed_low = blocked(group_pull(grad_grouped.reshape(length, heads, VD))[0].astype(bf16))
    grad_attn = jnp.einsum(
        "bthv,bshv->bhts", grad_mixed_low, value_low, preferred_element_type=f32
    )
    grad_scores_low = (grad_attn * within).astype(bf16)
    grad_query = jnp.einsum(
        "bhts,bshd->bthd", grad_scores_low, key_low, preferred_element_type=f32
    )
    grad_query = (
        grad_query
        + jnp.einsum("bthv,bhdv->bthd", grad_mixed_low, state_low, preferred_element_type=f32)
        * reach[..., None]
    )
    grad_key = jnp.einsum(
        "bhts,bthd->bshd", grad_scores_low, query_low, preferred_element_type=f32
    )
    grad_value = jnp.einsum(
        "bhts,bthv->bshv", attn_low, grad_mixed_low, preferred_element_type=f32
    )
    grad_state = jnp.einsum(
        "bthd,bthv->bhdv",
        query_low.astype(f32) * reach[..., None],
        grad_mixed_low.astype(f32),
        precision=highest,
    )
    leave = jnp.zeros_like(grad_state[0])
    leaves = [None] * n_seq
    for b in reversed(range(n_seq)):
        leaves[b] = leave
        leave = grad_state[b] + carry[b][:, None, None] * leave
    grad_own = jnp.stack(leaves)
    grad_key = (
        grad_key
        + jnp.einsum("bthv,bhdv->bthd", value_wide, grad_own, precision=highest)
        * ending[..., None]
    )
    grad_value = grad_value + jnp.einsum("bthd,bhdv->bthv", key_scaled, grad_own, precision=highest)
    grad_v_low = grad_value.reshape(length, heads * VD).astype(bf16)
    g_v = weight_grad(first_low, grad_v_low)
    grad_query_raw = rotate_pull(grad_query.reshape(length, heads * QK))[0]
    grad_key_raw = rotate_pull(grad_key.reshape(length, heads * QK))[0]
    grad_qk_low = jnp.concatenate([grad_query_raw.astype(bf16), grad_key_raw.astype(bf16)], axis=1)
    grad_first = row_scatter(
        contract_last(grad_qk_low, w_qk)
        + contract_last(grad_v_low, w_v)
        + contract_last(grad_gate_low, w_g)
    )
    g_qk = weight_grad(first_low, grad_qk_low)
    grad_input_ln, gain_one, bias_one = first_pull(grad_first)
    grad_tokens = grad_hidden + grad_input_ln
    grad_weights = jnp.concatenate(
        [
            spread(g_qk[:, : heads * QK]),
            spread(g_qk[:, heads * QK :]),
            spread(g_v),
            spread(g_g),
            spread(g_in),
            spread(g_out),
            spread(g_down),
        ],
        axis=1,
    )
    grad_gain, grad_bias = lax.psum(
        (jnp.stack([gain_one, gain_two]), jnp.stack([bias_one, bias_two])), ("dp", "seq")
    )
    return (result, grad_tokens, grad_weights, grad_gain, grad_bias)


def solution(mesh):
    placed = (
        P(("dp", "seq"), None),
        P("dp", None),
        P(),
        P(),
        P("dp", None),
        P(("dp", "seq"), None),
    )
    divides = HEADS % mesh.shape["seq"] == 0
    return jax.shard_map(
        per_device_heads if divides else per_device_spread,
        mesh=mesh,
        in_specs=placed,
        out_specs=(
            P(("dp", "seq"), None),
            P(("dp", "seq"), None),
            P(("dp", "seq"), None),
            P(),
            P(),
        ),
        check_vma=False,
    )
```

```python
import functools

import jax
import jax.numpy as jnp
from jax import lax
from jax.experimental import pallas as pl
from jax.experimental.pallas import tpu as pltpu
from jax.sharding import PartitionSpec as P

HEADS = 8
QK = 256
VD = 512
FF = 4096


norm_eps = 1e-05
highest = lax.Precision.HIGHEST
f32 = jnp.float32
bf16 = jnp.bfloat16


def prefix(x, axis, combine, identity, reverse):
    devices, place = (lax.axis_size(axis), lax.axis_index(axis))
    everything = jax.tree.map(lambda part: lax.all_gather(part, axis), x)
    start = jax.tree.map(
        lambda part, zero: jnp.broadcast_to(jnp.asarray(zero, part.dtype), part.shape), x, identity
    )

    def step(k, before):
        at = devices - 1 - k if reverse else k
        reached = at > place if reverse else at < place
        new = combine(before, jax.tree.map(lambda part: part[at], everything))
        return jax.tree.map(lambda a, b: jnp.where(reached, a, b), new, before)

    return lax.fori_loop(0, devices, step, start)


def layer_norm(values, gain, shift):
    centre = jnp.mean(values, axis=-1, keepdims=True)
    centred = values - centre
    spread = jnp.mean(centred * centred, axis=-1, keepdims=True)
    return centred * lax.rsqrt(spread + norm_eps) * gain + shift


def group_norm(values):
    centre = jnp.mean(values, axis=-1, keepdims=True)
    centred = values - centre
    spread = jnp.mean(centred * centred, axis=-1, keepdims=True)
    return centred * lax.rsqrt(spread + norm_eps)


def gelu_tanh(values):
    return jax.nn.gelu(values, approximate=True)


def gating(gate_values, normed):
    return jax.nn.silu(gate_values) * normed


def rotate(values, positions, heads_count):
    length = values.shape[0]
    shaped = values.reshape(length, heads_count, -1)
    half_size = shaped.shape[-1] // 2
    inverse = 10000.0 ** (-(jnp.arange(half_size, dtype=jnp.float32) / half_size))
    angles = positions.astype(jnp.float32)[:, None] * inverse[None, :]
    cosine = jnp.cos(angles)[:, None, :]
    sine = jnp.sin(angles)[:, None, :]
    front = shaped[..., :half_size]
    back_half = shaped[..., half_size:]
    turned = jnp.concatenate(
        [front * cosine - back_half * sine, back_half * cosine + front * sine], axis=-1
    )
    return turned.reshape(length, -1)


def head_logs():
    return jnp.log1p(-(2.0 ** (-5.0 - jnp.arange(HEADS, dtype=jnp.float32))))


def decay_tables(segs, seg_prev, logs):
    length = segs.shape[0]
    local = jnp.arange(length, dtype=jnp.int32)
    gap = (local[:, None] - local[None, :]).astype(jnp.float32)
    same = (segs[:, None] == segs[None, :]) & (local[:, None] >= local[None, :])
    within = jnp.where(
        same[None], jnp.exp(jnp.where(same[None], gap[None] * logs[:, None, None], 0.0)), 0.0
    )
    reach = jnp.where(
        (segs == seg_prev)[None, :],
        jnp.exp((local + 1).astype(jnp.float32)[None, :] * logs[:, None]),
        0.0,
    )
    ending = jnp.where(
        (segs == segs[-1])[None, :],
        jnp.exp((length - 1 - local).astype(jnp.float32)[None, :] * logs[:, None]),
        0.0,
    )
    carry = jnp.where(segs[-1] == seg_prev, jnp.exp(length * logs), 0.0)
    return (within, reach.T, ending.T, carry)


def combine_states(earlier, later):
    return (later[0] + later[1][:, None, None] * earlier[0], earlier[1] * later[1])


def contract_last(left, right):
    return lax.dot_general(
        left, right, (((1,), (1,)), ((), ())), preferred_element_type=jnp.float32
    )


def per_device_spread(tokens, weights, ln_gain, ln_bias, doc_starts, cotangent):
    full = lax.all_gather(weights, "dp", axis=0, tiled=True)
    query_width = HEADS * QK
    value_width = HEADS * VD
    mixer_cols = 2 * query_width + 2 * value_width
    ffn_end = mixer_cols + FF
    out_end = ffn_end + value_width
    block = tokens.shape[0]
    offset = lax.axis_index("seq") * block
    positions = offset + jnp.arange(block, dtype=jnp.int32)
    starts = doc_starts[0]
    segs = jnp.sum((starts[None, :] <= positions[:, None]).astype(jnp.int32), axis=1)
    seg_prev = jnp.sum((starts <= offset - 1).astype(jnp.int32))
    within, reach, ending, carry = decay_tables(segs, seg_prev, head_logs())
    inputs = tokens.astype(jnp.float32)
    first, first_pull = jax.vjp(layer_norm, inputs, ln_gain[0], ln_bias[0])
    first_low = first.astype(jnp.bfloat16)
    project = jnp.dot(first_low, full[:, :mixer_cols], preferred_element_type=jnp.float32)

    def rotate_here(values):
        return rotate(values, positions, HEADS)

    query_rot, rotate_pull = jax.vjp(rotate_here, project[:, :query_width])
    query_low = query_rot.astype(jnp.bfloat16).reshape(block, HEADS, QK)
    key_low = (
        rotate_here(project[:, query_width : 2 * query_width])
        .astype(jnp.bfloat16)
        .reshape(block, HEADS, QK)
    )
    value_low = (
        project[:, 2 * query_width : 2 * query_width + value_width]
        .astype(jnp.bfloat16)
        .reshape(block, HEADS, VD)
    )
    gate_raw = project[:, 2 * query_width + value_width : mixer_cols]
    scores = jnp.einsum("thd,shd->hts", query_low, key_low, preferred_element_type=jnp.float32)
    attn_low = (scores * within).astype(jnp.bfloat16)
    intra = jnp.einsum("hts,shv->thv", attn_low, value_low, preferred_element_type=jnp.float32)
    key_scaled = key_low.astype(jnp.float32) * ending[:, :, None]
    value_wide = value_low.astype(jnp.float32)
    own_state = jnp.einsum("thd,thv->hdv", key_scaled, value_wide, precision=highest)
    incoming = prefix(
        (own_state, carry),
        "seq",
        combine_states,
        (jnp.zeros_like(own_state), jnp.ones_like(carry)),
        False,
    )[0]
    state_low = incoming.astype(jnp.bfloat16)
    across = (
        jnp.einsum("thd,hdv->thv", query_low, state_low, preferred_element_type=jnp.float32)
        * reach[:, :, None]
    )
    mixed = intra + across
    grouped, group_pull = jax.vjp(group_norm, mixed)
    gated, gating_pull = jax.vjp(gating, gate_raw, grouped.reshape(block, value_width))
    gated_low = gated.astype(jnp.bfloat16)
    hidden = inputs + contract_last(gated_low, full[:, ffn_end:out_end])
    second, second_pull = jax.vjp(layer_norm, hidden, ln_gain[1], ln_bias[1])
    second_low = second.astype(jnp.bfloat16)
    inner = jnp.dot(second_low, full[:, mixer_cols:ffn_end], preferred_element_type=jnp.float32)
    active, active_pull = jax.vjp(gelu_tanh, inner)
    active_low = active.astype(jnp.bfloat16)
    result = (hidden + contract_last(active_low, full[:, out_end:])).astype(jnp.bfloat16)
    grad_active = jnp.dot(cotangent, full[:, out_end:], preferred_element_type=jnp.float32)
    grad_inner_low = active_pull(grad_active)[0].astype(jnp.bfloat16)
    grad_second = contract_last(grad_inner_low, full[:, mixer_cols:ffn_end])
    grad_hidden_ln, gain_two, bias_two = second_pull(grad_second)
    grad_hidden = cotangent.astype(jnp.float32) + grad_hidden_ln
    grad_branch_low = grad_hidden.astype(jnp.bfloat16)
    grad_gated = jnp.dot(
        grad_branch_low, full[:, ffn_end:out_end], preferred_element_type=jnp.float32
    )
    grad_gate, grad_grouped = gating_pull(grad_gated)
    grad_mixed_low = group_pull(grad_grouped.reshape(block, HEADS, VD))[0].astype(jnp.bfloat16)
    grad_attn = jnp.einsum(
        "thv,shv->hts", grad_mixed_low, value_low, preferred_element_type=jnp.float32
    )
    grad_scores_low = (grad_attn * within).astype(jnp.bfloat16)
    grad_query = jnp.einsum(
        "hts,shd->thd", grad_scores_low, key_low, preferred_element_type=jnp.float32
    )
    grad_query = (
        grad_query
        + jnp.einsum("thv,hdv->thd", grad_mixed_low, state_low, preferred_element_type=jnp.float32)
        * reach[:, :, None]
    )
    grad_key = jnp.einsum(
        "hts,thd->shd", grad_scores_low, query_low, preferred_element_type=jnp.float32
    )
    grad_value = jnp.einsum(
        "hts,thv->shv", attn_low, grad_mixed_low, preferred_element_type=jnp.float32
    )
    grad_state = jnp.einsum(
        "thd,thv->hdv",
        query_low.astype(jnp.float32) * reach[:, :, None],
        grad_mixed_low.astype(jnp.float32),
        precision=highest,
    )
    grad_own = prefix(
        (grad_state, carry),
        "seq",
        combine_states,
        (jnp.zeros_like(grad_state), jnp.ones_like(carry)),
        True,
    )[0]
    grad_key = (
        grad_key
        + jnp.einsum("thv,hdv->thd", value_wide, grad_own, precision=highest) * ending[:, :, None]
    )
    grad_value = grad_value + jnp.einsum("thd,hdv->thv", key_scaled, grad_own, precision=highest)
    grad_query_raw = rotate_pull(grad_query.reshape(block, query_width))[0]
    grad_key_raw = rotate_pull(grad_key.reshape(block, query_width))[0]
    grad_project_low = jnp.concatenate(
        [
            grad_query_raw.astype(jnp.bfloat16),
            grad_key_raw.astype(jnp.bfloat16),
            grad_value.reshape(block, value_width).astype(jnp.bfloat16),
            grad_gate.astype(jnp.bfloat16),
        ],
        axis=1,
    )
    grad_first = contract_last(grad_project_low, full[:, :mixer_cols])
    grad_input_ln, gain_one, bias_one = first_pull(grad_first)
    grad_tokens = grad_hidden + grad_input_ln
    contract = (((0,), (0,)), ((), ()))
    pieces = [
        lax.dot_general(first_low, grad_project_low, contract, preferred_element_type=jnp.float32),
        lax.dot_general(second_low, grad_inner_low, contract, preferred_element_type=jnp.float32),
        lax.dot_general(grad_branch_low, gated_low, contract, preferred_element_type=jnp.float32),
        lax.dot_general(cotangent, active_low, contract, preferred_element_type=jnp.float32),
    ]
    grad_weights = lax.psum_scatter(
        jnp.concatenate(pieces, axis=1), ("dp", "seq"), scatter_dimension=0, tiled=True
    )
    grad_gain, grad_bias = lax.psum(
        (jnp.stack([gain_one, gain_two]), jnp.stack([bias_one, bias_two])), ("dp", "seq")
    )
    return (result, grad_tokens, grad_weights, grad_gain, grad_bias)


MESH = pl.DeviceIdType.MESH
ANY = pl.BlockSpec(memory_space=pl.ANY)
DMA = pltpu.SemaphoreType.DMA


def cost(flops, moved):
    return pl.CostEstimate(flops=int(flops), bytes_accessed=int(moved), transcendentals=0)


def flipped(index, size):
    return index + size * (1 - 2 * ((index // size) % 2))


def row_peers():
    me = lax.axis_index("seq")
    return me, flipped(me, 1), flipped(me, 2), flipped(me, 4)


def greet(others):
    barrier = pltpu.get_barrier_semaphore()
    for axis, other in others:
        pl.semaphore_signal(barrier, inc=1, device_id={axis: other}, device_id_type=MESH)
    pl.semaphore_wait(barrier, len(others))


def seq_copy(src, dst, send, recv, target):
    return pltpu.make_async_remote_copy(
        src_ref=src,
        dst_ref=dst,
        send_sem=send,
        recv_sem=recv,
        device_id={"seq": target},
        device_id_type=MESH,
    )


def gather_kernel(chunks, own, out, send, recv, local):
    me, core, along, across = row_peers()
    corner = along + across - me
    rows = own.shape[0] // chunks
    half = chunks // 2
    greet([("seq", core), ("seq", along), ("seq", across)])

    def copy(lane, k, who, target):
        part = pl.ds(k * rows, rows)
        src = own.at[part] if lane in (0, 1, 4) else out.at[who, part]
        return seq_copy(src, out.at[who, part], send.at[lane, k], recv.at[lane, k], target)

    mine = pltpu.make_async_copy(own, out.at[me], local)
    mine.start()
    started = []

    def go(one):
        one.start()
        started.append(one)

    order_along = list(range(chunks))
    order_across = order_along[half:] + order_along[:half]
    for i in range(chunks):
        go(copy(0, order_along[i], me, along))
        go(copy(1, order_across[i], me, across))
        go(copy(4, order_along[i], me, core))
    for i in range(chunks):
        k = order_along[i]
        copy(0, k, along, along).wait_recv()
        if k < half:
            go(copy(3, k, along, across))
        go(copy(5, k, along, core))
        k = order_across[i]
        copy(1, k, across, across).wait_recv()
        if k >= half:
            go(copy(2, k, across, along))
        go(copy(6, k, across, core))
    for k in range(half):
        copy(3, k, corner, across).wait_recv()
        go(copy(7, k, corner, core))
        copy(2, half + k, corner, along).wait_recv()
        go(copy(7, half + k, corner, core))
    turn = core - me
    for k in range(chunks):
        copy(4, k, core, core).wait_recv()
        copy(5, k, along + turn, core).wait_recv()
        copy(6, k, across + turn, core).wait_recv()
        copy(7, k, corner + turn, core).wait_recv()
    for one in started:
        one.wait_send()
    mine.wait()


def row_gather(own, ident, chunks=8):
    shape = (8,) + own.shape
    out = pl.pallas_call(
        functools.partial(gather_kernel, chunks),
        out_shape=jax.ShapeDtypeStruct(shape, own.dtype),
        in_specs=[ANY],
        out_specs=ANY,
        scratch_shapes=[DMA((8, chunks)), DMA((8, chunks)), DMA],
        compiler_params=pltpu.CompilerParams(collective_id=ident, has_side_effects=True),
        cost_estimate=cost(0, 120e6),
        name=f"row_gather_{ident}",
    )(own)
    return out.reshape((8 * own.shape[0],) + own.shape[1:])


def scatter_kernel(tile, exact, left, right, *refs):
    if exact:
        few, out, few_out, *refs, few_recv, few_sems = refs
    else:
        out, *refs = refs
    core_send, core_recv, far_send, far_recv, near_send, near_recv, wide, *refs = refs
    core_sems, far_sems, near_sems = refs
    me, core, along, across = row_peers()
    corner = along + across - me
    turn = core - me
    rows = out.shape[0]
    half = rows // 2
    tiles = out.shape[1] // tile
    greet([("seq", core), ("seq", along), ("seq", across)])
    halves = (pl.ds(0, half), pl.ds(half, half))

    def few_copy(i):
        return seq_copy(
            few_out, few_recv.at[i], few_sems.at[0, i], few_sems.at[1, i], (core, along, across)[i]
        )

    def few_step(i):
        if exact:
            few_copy(i).wait()
            few_out[...] += few_recv[i]
            if i < 2:
                few_copy(i + 1).start()

    def product(block, sink):
        at = pl.ds(pl.multiple_of(block * rows, rows), rows)

        @pl.loop(0, tiles)
        def _(i):
            cols = pl.ds(pl.multiple_of(i * tile, tile), tile)
            sink(cols, contract_last(left[at, :], right[cols, :]))

    def core_copy(i):
        return seq_copy(
            core_send.at[i], core_recv.at[i], core_sems.at[0, i], core_sems.at[1, i], core
        )

    def far_copy(i):
        return seq_copy(
            far_send.at[halves[i]],
            far_recv.at[halves[i]],
            far_sems.at[0, i],
            far_sems.at[1, i],
            (along, across)[i],
        )

    def near_copy(i, part):
        return seq_copy(
            near_send.at[i, halves[part]],
            near_recv.at[i, halves[part]],
            near_sems.at[0, 2 * i + part],
            near_sems.at[1, 2 * i + part],
            (along, across)[i],
        )

    def for_core(i, block):
        def sink(cols, value):
            core_send[i, :, cols] = value.astype(bf16)

        product(block, sink)
        core_copy(i).start()

    def near(i, block):
        core_copy(1 + i).wait_recv()
        ready, late = (0, 1) if i == 0 else (1, 0)

        def sink(cols, value):
            total = value + core_recv[1 + i, :, cols].astype(f32)
            near_send[i, halves[ready], cols] = total[ready * half : (ready + 1) * half].astype(bf16)
            wide[i, :, cols] = total[late * half : (late + 1) * half]

        product(block, sink)
        near_copy(i, ready).start()

    def near_late(i):
        late = 1 if i == 0 else 0
        far_copy(late).wait_recv()

        @pl.loop(0, tiles)
        def _(t):
            cols = pl.ds(pl.multiple_of(t * tile, tile), tile)
            total = wide[i, :, cols] + far_recv[halves[late], cols].astype(f32)
            near_send[i, halves[late], cols] = total.astype(bf16)

        near_copy(i, late).start()

    if exact:

        @pl.loop(0, tiles)
        def _(i):
            cols = pl.ds(pl.multiple_of(i * tile, tile), tile)
            few_out[:, cols] = contract_last(few[...], right[cols, :])

        few_copy(0).start()

    for_core(0, corner + turn)
    for_core(1, along + turn)
    core_copy(0).wait_recv()

    def far_sink(cols, value):
        far_send[:, cols] = (value + core_recv[0, :, cols].astype(f32)).astype(bf16)

    product(corner, far_sink)
    far_copy(0).start()
    far_copy(1).start()
    for_core(2, across + turn)
    few_step(0)
    near(0, along)
    few_step(1)
    near(1, across)
    few_step(2)
    for_core(3, core)
    core_copy(3).wait_recv()

    def own_sink(cols, value):
        out[:, cols] = value + core_recv[3, :, cols].astype(f32)

    product(me, own_sink)
    near_late(0)
    near_late(1)
    for part, i in ((0, 0), (1, 1), (1, 0), (0, 1)):
        near_copy(i, part).wait_recv()

        @pl.loop(0, tiles)
        def _(t):
            cols = pl.ds(pl.multiple_of(t * tile, tile), tile)
            out[halves[part], cols] += near_recv[i, halves[part], cols].astype(f32)

    for i in range(4):
        core_copy(i).wait_send()
    for i in range(2):
        far_copy(i).wait_send()
        near_copy(i, 0).wait_send()
        near_copy(i, 1).wait_send()


def row_scatter(left, right, ident, column=0, tile=512, few=None):
    depth = left.shape[1]
    rows, width = left.shape[0] // 8, right.shape[0]
    whole = pltpu.VMEM
    exact = few is not None
    extra_in, extra_out, extra_scratch = [], [], []
    shapes = [jax.ShapeDtypeStruct((rows, width), f32)]
    if exact:
        count = few.shape[0]
        extra_in = [pl.BlockSpec((count, depth), lambda i: (0, 0))]
        extra_out = [pl.BlockSpec((count, width), lambda i: (0, 0))]
        extra_scratch = [whole((3, count, width), f32), DMA((2, 3))]
        shapes.append(jax.ShapeDtypeStruct((count, width), f32))
    out = pl.pallas_call(
        functools.partial(scatter_kernel, tile, exact),
        out_shape=shapes,
        grid=(1,),
        in_specs=[
            pl.BlockSpec((8 * rows, depth), lambda i: (0, 0), pipeline_mode=pl.Buffered(1)),
            pl.BlockSpec((width, depth), lambda i: (0, column), pipeline_mode=pl.Buffered(1)),
        ]
        + extra_in,
        out_specs=[pl.BlockSpec((rows, width), lambda i: (0, 0), pipeline_mode=pl.Buffered(1))]
        + extra_out,
        scratch_shapes=[
            whole((4, rows, width), bf16),
            whole((4, rows, width), bf16),
            whole((rows, width), bf16),
            whole((rows, width), bf16),
            whole((2, rows, width), bf16),
            whole((2, rows, width), bf16),
            whole((2, rows // 2, width), f32),
            DMA((2, 4)),
            DMA((2, 2)),
            DMA((2, 4)),
        ]
        + extra_scratch,
        compiler_params=pltpu.CompilerParams(
            collective_id=ident, has_side_effects=True, vmem_limit_bytes=48 * 2**20
        ),
        cost_estimate=cost(16 * rows * depth * width, 120e6),
        name=f"row_scatter_{ident}",
    )(*([left, right] + ([few] if exact else [])))
    return out if exact else out[0]


def exchange_kernel(widths, grad, *refs):
    outs, (send, recv, local) = refs[: len(widths)], refs[len(widths) :]
    me = lax.axis_index("seq")
    rows = outs[0].shape[0]
    others = []
    for step in range(8):
        other = me
        for size in (1, 2, 4):
            if step & size:
                other = flipped(other, size)
        others.append(other)
    greet([("seq", other) for other in others[1:]])
    started = []
    for step in (6, 7, 2, 3, 4, 5, 1, 0):
        other = others[step]
        at = pl.ds(pl.multiple_of(other * rows, rows), rows)
        start = 0
        for i, width in enumerate(widths):
            src = grad.at[at, pl.ds(start, width)]
            dst = outs[i].at[:, pl.ds(pl.multiple_of(me * width, width), width)]
            start += width
            if step == 0:
                one = pltpu.make_async_copy(src, dst, local.at[i])
            else:
                one = seq_copy(src, dst, send.at[step, i], recv.at[step, i], other)
            one.start()
            started.append(one)
    for one in started:
        one.wait()


def row_exchange(grad, widths, ident):
    rows = grad.shape[0] // 8
    n = len(widths)
    return pl.pallas_call(
        functools.partial(exchange_kernel, widths),
        out_shape=[jax.ShapeDtypeStruct((rows, 8 * width), grad.dtype) for width in widths],
        in_specs=[ANY],
        out_specs=[ANY] * n,
        scratch_shapes=[DMA((8, n)), DMA((8, n)), DMA((n,))],
        compiler_params=pltpu.CompilerParams(collective_id=ident, has_side_effects=True),
        cost_estimate=cost(0, 30e6),
        name=f"row_exchange_{ident}",
    )(grad)


def total_kernel(stages, own, out, held, send, recv):
    places = {axis: lax.axis_index(axis) for axis, _ in stages}
    partners = [(axis, flipped(places[axis], size)) for axis, size in stages]
    greet(partners)
    out[...] = own[...]
    for i, (axis, other) in enumerate(partners):
        copy = pltpu.make_async_remote_copy(
            src_ref=out,
            dst_ref=held.at[i],
            send_sem=send.at[i],
            recv_sem=recv.at[i],
            device_id={axis: other},
            device_id_type=MESH,
        )
        copy.start()
        copy.wait()
        out[...] += held[i]


def device_total(own, dp_size, ident):
    stages = [("seq", 1), ("seq", 2), ("seq", 4)]
    size = 1
    while size < dp_size:
        stages.append(("dp", size))
        size *= 2
    n = len(stages)
    return pl.pallas_call(
        functools.partial(total_kernel, stages),
        out_shape=jax.ShapeDtypeStruct(own.shape, f32),
        in_specs=[pl.BlockSpec(memory_space=pltpu.VMEM)],
        out_specs=pl.BlockSpec(memory_space=pltpu.VMEM),
        scratch_shapes=[pltpu.VMEM((n,) + own.shape, f32), DMA((n,)), DMA((n,))],
        compiler_params=pltpu.CompilerParams(collective_id=ident, has_side_effects=True),
        cost_estimate=cost(0, 30e6),
        name=f"device_total_{ident}",
    )(own)


def sections(n_seq):
    widths = (HEADS * QK, HEADS * QK, HEADS * VD, HEADS * VD, FF, HEADS * VD, FF)
    start, out = 0, []
    for width in widths:
        out.append((start, width // n_seq))
        start += width
    return out


def per_device_heads(tokens, weights, ln_gain, ln_bias, doc_starts, cotangent):
    n_seq, place = lax.axis_size("seq"), lax.axis_index("seq")
    heads = HEADS // n_seq
    block = tokens.shape[0]
    length = block * n_seq
    secs = sections(n_seq)

    def gather_weights(which):
        part = jnp.concatenate(
            [
                lax.dynamic_slice_in_dim(weights, start + place * width, width, axis=1)
                for start, width in (secs[i] for i in which)
            ],
            axis=1,
        )
        return lax.all_gather(part, "dp", axis=0, tiled=True)

    mix = gather_weights((0, 1, 2, 3))
    w_out = gather_weights((5,))
    ffn = gather_weights((4, 6))
    ffn_width = FF // n_seq
    q_end, k_end = heads * QK, 2 * heads * QK
    v_end = k_end + heads * VD

    positions = jnp.arange(length, dtype=jnp.int32)
    starts = doc_starts[0]
    segs = jnp.sum((starts[None, :] <= positions[:, None]).astype(jnp.int32), axis=1)
    seg_blocks = segs.reshape(n_seq, block)
    seg_before = jnp.concatenate([jnp.zeros((1,), jnp.int32), seg_blocks[:-1, -1]])
    inputs = tokens.astype(f32)
    first, first_pull = jax.vjp(layer_norm, inputs, ln_gain[0], ln_bias[0])
    first_low = row_gather(first.astype(bf16), 1)
    cot_low = row_gather(cotangent, 2)
    project = jnp.dot(first_low, mix, preferred_element_type=f32)

    def rotate_here(values):
        return rotate(values, positions, heads)

    query_rot, rotate_pull = jax.vjp(rotate_here, project[:, :q_end])

    def blocked(values):
        return values.reshape(n_seq, block, heads, -1)

    query_low = blocked(query_rot.astype(bf16))
    key_low = blocked(rotate_here(project[:, q_end:k_end]).astype(bf16))
    value_low = blocked(project[:, k_end:v_end].astype(bf16))
    gate_raw = project[:, v_end:]
    logs = lax.dynamic_slice_in_dim(head_logs(), place * heads, heads)
    within, reach, ending, carry = jax.vmap(decay_tables, (0, 0, None))(
        seg_blocks, seg_before, logs
    )
    scores = jnp.einsum("bthd,bshd->bhts", query_low, key_low, preferred_element_type=f32)
    attn_low = (scores * within).astype(bf16)
    intra = jnp.einsum("bhts,bshv->bthv", attn_low, value_low, preferred_element_type=f32)
    key_scaled = key_low.astype(f32) * ending[..., None]
    value_wide = value_low.astype(f32)
    own_state = jnp.einsum("bthd,bthv->bhdv", key_scaled, value_wide, precision=highest)
    state = jnp.zeros_like(own_state[0])
    states = []
    for b in range(n_seq):
        states.append(state.astype(bf16))
        state = own_state[b] + carry[b][:, None, None] * state
    state_low = jnp.stack(states)
    across = (
        jnp.einsum("bthd,bhdv->bthv", query_low, state_low, preferred_element_type=f32)
        * reach[..., None]
    )
    mixed = (intra + across).reshape(length, heads, VD)
    grouped, group_pull = jax.vjp(group_norm, mixed)
    gated, gating_pull = jax.vjp(gating, gate_raw, grouped.reshape(length, heads * VD))
    gated_low = gated.astype(bf16)
    local = place * block + jnp.arange(block, dtype=jnp.int32)
    some = jnp.tile(starts, 4)
    picks = (some[:, None] == positions[None, :]).astype(bf16)

    def few_rows(values):
        return jnp.dot(picks, values, preferred_element_type=f32).astype(bf16)

    def exact_scatter(left, right, ident):
        out, few = row_scatter(left, right, ident, few=few_rows(left))
        for i in range(starts.shape[0]):
            out = jnp.where((local == starts[i])[:, None], few[i][None, :], out)
        return out

    hidden = inputs + exact_scatter(gated_low, w_out, 3)
    second, second_pull = jax.vjp(layer_norm, hidden, ln_gain[1], ln_bias[1])
    second_low = row_gather(second.astype(bf16), 4)
    inner = jnp.dot(second_low, ffn[:, :ffn_width], preferred_element_type=f32)
    active, active_pull = jax.vjp(gelu_tanh, inner)
    active_low = active.astype(bf16)
    contract = (((0,), (0,)), ((), ()))

    def product(left, right):
        return lax.dot_general(left, right, contract, preferred_element_type=f32).astype(bf16)

    def reduce_dp(grads):
        return lax.psum_scatter(
            jnp.concatenate(grads, axis=1), "dp", scatter_dimension=0, tiled=True
        )

    grad_active = jnp.dot(cot_low, ffn[:, ffn_width:], preferred_element_type=f32)
    grad_inner_low = active_pull(grad_active)[0].astype(bf16)
    ffn_grads, grad_inner_low, active_low = lax.optimization_barrier(
        (
            jnp.concatenate(
                [product(second_low, grad_inner_low), product(cot_low, active_low)], axis=1
            ),
            grad_inner_low,
            active_low,
        )
    )
    ffn_grads = reduce_dp([ffn_grads])
    grad_second = exact_scatter(grad_inner_low, ffn, 5)
    grad_hidden_ln, gain_two, bias_two = second_pull(grad_second)
    grad_hidden = cotangent.astype(f32) + grad_hidden_ln
    grad_branch_low = row_gather(grad_hidden.astype(bf16), 6)
    grad_gated = jnp.dot(grad_branch_low, w_out, preferred_element_type=f32)
    grad_gate, grad_grouped = gating_pull(grad_gated)
    grad_gate_low = grad_gate.astype(bf16)
    side_grads, ffn_grads = lax.optimization_barrier(
        (
            jnp.concatenate(
                [product(first_low, grad_gate_low), product(grad_branch_low, gated_low)], axis=1
            ),
            ffn_grads,
        )
    )
    side_grads = reduce_dp([side_grads])
    grad_mixed_low = blocked(group_pull(grad_grouped.reshape(length, heads, VD))[0].astype(bf16))
    grad_attn = jnp.einsum(
        "bthv,bshv->bhts", grad_mixed_low, value_low, preferred_element_type=f32
    )
    grad_scores_low = (grad_attn * within).astype(bf16)
    grad_query = jnp.einsum(
        "bhts,bshd->bthd", grad_scores_low, key_low, preferred_element_type=f32
    )
    grad_query = (
        grad_query
        + jnp.einsum("bthv,bhdv->bthd", grad_mixed_low, state_low, preferred_element_type=f32)
        * reach[..., None]
    )
    grad_key = jnp.einsum(
        "bhts,bthd->bshd", grad_scores_low, query_low, preferred_element_type=f32
    )
    grad_value = jnp.einsum(
        "bhts,bthv->bshv", attn_low, grad_mixed_low, preferred_element_type=f32
    )
    grad_state = jnp.einsum(
        "bthd,bthv->bhdv",
        query_low.astype(f32) * reach[..., None],
        grad_mixed_low.astype(f32),
        precision=highest,
    )
    leave = jnp.zeros_like(grad_state[0])
    leaves = [None] * n_seq
    for b in reversed(range(n_seq)):
        leaves[b] = leave
        leave = grad_state[b] + carry[b][:, None, None] * leave
    grad_own = jnp.stack(leaves)
    grad_key = (
        grad_key
        + jnp.einsum("bthv,bhdv->bthd", value_wide, grad_own, precision=highest)
        * ending[..., None]
    )
    grad_value = grad_value + jnp.einsum("bthd,bhdv->bthv", key_scaled, grad_own, precision=highest)
    grad_v_low = grad_value.reshape(length, heads * VD).astype(bf16)
    grad_query_raw = rotate_pull(grad_query.reshape(length, heads * QK))[0]
    grad_key_raw = rotate_pull(grad_key.reshape(length, heads * QK))[0]
    grad_project_low = jnp.concatenate(
        [grad_query_raw.astype(bf16), grad_key_raw.astype(bf16), grad_v_low, grad_gate_low], axis=1
    )
    qkv_grads, grad_project_low, active_low = lax.optimization_barrier(
        (product(first_low, grad_project_low[:, :v_end]), grad_project_low, active_low)
    )
    qkv_grads = reduce_dp([qkv_grads])
    grad_first = row_scatter(grad_project_low, mix, 7)
    grad_input_ln, gain_one, bias_one = first_pull(grad_first)
    grad_tokens = grad_hidden + grad_input_ln
    result = (hidden + row_scatter(active_low, ffn, 8, column=1)).astype(bf16)
    g_in, g_down = row_exchange(ffn_grads, (ffn_width, ffn_width), 9)
    g_g, g_out = row_exchange(side_grads, (heads * VD, heads * VD), 10)
    g_q, g_k, g_v = row_exchange(qkv_grads, (heads * QK, heads * QK, heads * VD), 12)
    grad_weights = jnp.concatenate([g_q, g_k, g_v, g_g, g_in, g_out, g_down], axis=1).astype(f32)
    norms = device_total(
        jnp.stack([gain_one, gain_two, bias_one, bias_two] * 2), lax.axis_size("dp"), 13
    )
    grad_gain, grad_bias = norms[:2], norms[2:4]
    return (result, grad_tokens, grad_weights, grad_gain, grad_bias)


def solution(mesh):
    placed = (
        P(("dp", "seq"), None),
        P("dp", None),
        P(),
        P(),
        P("dp", None),
        P(("dp", "seq"), None),
    )
    dp_size = mesh.shape["dp"]
    fits = mesh.shape["seq"] == HEADS == 8 and dp_size & (dp_size - 1) == 0
    return jax.shard_map(
        per_device_heads if fits else per_device_spread,
        mesh=mesh,
        in_specs=placed,
        out_specs=(
            P(("dp", "seq"), None),
            P(("dp", "seq"), None),
            P(("dp", "seq"), None),
            P(),
            P(),
        ),
        check_vma=False,
    )
```
